256 devices in a mesh: dp: 16 (over x, y), col: 16 (over z, core).
Axes of the slice: x: 4, y: 4, z: 8, core: 2. Of those that a mesh axis runs over, the one named last changes fastest.
Arguments:
- activations: bfloat16 [16, 1024, 4096], P('dp', 'col'), may hold values from -6 to 6
- out_grads: bfloat16 [16, 1024, 14336], P('dp', None, 'col'), may hold values from -0.0625 to 0.0625
- prev_factor: float32 [64, 14336], P(None, 'col'), may hold values from -0.046875 to 0.046875
Outputs:
- left_basis: float32 [64, 4096], replicated
- right_factor: float32 [64, 14336], P(None, 'col')
- residual: bfloat16 [16, 4096, 14336], P('dp', None, 'col')
The draws below stay inside these ranges and needn't reach their ends.
All inputs are finite; a program needn't handle non-finite values.
Results may differ from the reference program's by a relative error of at most 0.00055.
Values may be sent and summed in bfloat16 or wider, within the bound.
A program may use at most 128 MiB of HBM per device.

```python
import jax
import jax.numpy as jnp
from jax import lax

D = 4096
FF = 14336
RANK = 64
GROUP_TOK = 1024
GROUPS = 16


def levels(key, dims, pieces, least, largest):
    level, own = 1.0, jax.random.fold_in(key, 6)
    for position, shards_of in pieces:
        steps = jnp.exp(jax.random.uniform(jax.random.fold_in(own, position), (shards_of,), jnp.float32, least / len(pieces), largest / len(pieces)))
        level = level * jnp.repeat(steps, dims[position] // shards_of).reshape([-1 if axis == position else 1 for axis in range(len(dims))])
    return level


def bell_draw(stream_key, extent, deviation, reach, shards=(), dtype=jnp.bfloat16):
    array = deviation * jax.random.normal(stream_key, extent, jnp.float32)
    if shards:
        array = array * levels(stream_key, extent, shards, -0.22, 0.18)
    return jnp.clip(array, -reach, reach).astype(dtype)


def setup_inputs(seed: int = 0) -> dict:
    arg_keys = jax.random.split(jax.random.key(seed), 4)
    activations = bell_draw(arg_keys[0], (GROUPS, GROUP_TOK, D), 1.0, 6.0, ((0, 16), (1, 16)))
    out_grads = bell_draw(arg_keys[1], (GROUPS, GROUP_TOK, FF), (8 * GROUP_TOK) ** -0.5, 0.0625, ((0, 16), (2, 16)))
    prev_factor = bell_draw(arg_keys[2], (RANK, FF), FF ** -0.5, 0.046875, ((1, 16),), jnp.float32)
    return dict(activations=activations, out_grads=out_grads, prev_factor=prev_factor)


def reference(activations, out_grads, prev_factor):
    groups = activations.shape[0]
    hi = lax.Precision.HIGHEST

    def group_sketch(pair):
        xg, dyg = pair
        proj = jnp.dot(dyg.astype(jnp.float32), prev_factor.T, precision=hi)
        return jnp.dot(proj.T, xg.astype(jnp.float32), precision=hi)
    sketch = jnp.sum(lax.map(group_sketch, (activations, out_grads)), axis=0) / groups
    gram = jnp.dot(sketch, sketch.T, precision=hi)
    factor = jnp.linalg.cholesky(gram)
    left_basis = lax.linalg.triangular_solve(factor, sketch, left_side=True, lower=True)

    def group_factor(pair):
        xg, dyg = pair
        proj = jnp.dot(left_basis, xg.astype(jnp.float32).T, precision=hi)
        return jnp.dot(proj, dyg.astype(jnp.float32), precision=hi)
    right_factor = jnp.sum(lax.map(group_factor, (activations, out_grads)), axis=0) / groups
    approx = jnp.dot(left_basis.T, right_factor, precision=hi)

    def group_residual(pair):
        xg, dyg = pair
        grad = jnp.dot(xg.T.astype(jnp.float32), dyg.astype(jnp.float32), preferred_element_type=jnp.float32)
        return (grad - approx).astype(jnp.bfloat16)
    residual = lax.map(group_residual, (activations, out_grads))
    return (left_basis, right_factor, residual)
```

```python
import functools

import jax
import jax.numpy as jnp
from jax import lax
from jax.experimental import pallas as pl
from jax.experimental.pallas import tpu as pltpu
from jax.sharding import PartitionSpec as P

MESH = pl.DeviceIdType.MESH
F32 = jnp.float32
BF16 = jnp.bfloat16
RANK = 64
HALF = 32
STAGES = ("rows", "proj", "zproj", "xysum", "zsum", "zgat", "xygat", "half", "zq", "xyfac", "xyfacg")


def split3(x):
    hi = x.astype(BF16)
    rest = x - hi.astype(F32)
    mid = rest.astype(BF16)
    lo = (rest - mid.astype(F32)).astype(BF16)
    return hi, mid, lo


def stack3(x):
    return jnp.concatenate(split3(x), axis=0)


def fold3(y, rows):
    return y[:rows] + (y[rows : 2 * rows] + y[2 * rows :])


NN = (((1,), (0,)), ((), ()))
NT = (((1,), (1,)), ((), ()))
TN = (((0,), (0,)), ((), ()))


def dot(a, b, dims):
    return lax.dot_general(a, b, dims, preferred_element_type=F32)


def inverse_factor(gram):
    n = gram.shape[0]
    row = lax.broadcasted_iota(jnp.int32, (n, n), 0)
    column = lax.broadcasted_iota(jnp.int32, (n, n), 1)
    eye = jnp.where(row == column, 1.0, 0.0).astype(F32)
    work = jnp.concatenate([eye, gram], axis=1)
    index = lax.broadcasted_iota(jnp.int32, (n, 1), 0)
    out = []
    for j in range(0, n, 2):
        r0, r1 = work[j : j + 1], work[j + 1 : j + 2]
        a = r0[:, n + j : n + j + 1]
        b = r0[:, n + j + 1 : n + j + 2]
        d = r1[:, n + j + 1 : n + j + 2]
        t = b / a
        s = d - b * t
        q1 = r1 - t * r0
        out.append(r0 * lax.rsqrt(a))
        out.append(q1 * lax.rsqrt(s))
        if j + 2 < n:
            c0 = work[:, n + j : n + j + 1]
            c1 = work[:, n + j + 1 : n + j + 2]
            below = index > j + 1
            m0 = jnp.where(below, c0 / a, 0.0)
            m1 = jnp.where(below, (c1 - c0 * t) / s, 0.0)
            work = work - m0 * r0 - m1 * q1
    return jnp.concatenate(out, axis=0)[:, :n]


def chain_kernel(
    groups, chips, a_ref, b_ref, p_ref, l_ref, r_ref,
    rows, halves, halves_in, psum, psum_in, part, part_in, tile, tile_in, tiles, full, qs, fac, fac_in, facs,
    *sems,
):
    send = dict(zip(STAGES, sems[: len(STAGES)]))
    recv = dict(zip(STAGES, sems[len(STAGES) : 2 * len(STAGES)]))
    local = sems[-1]
    g = lax.axis_index("dp")
    c = lax.axis_index("col")
    z, k = c // 2, c % 2
    wide = part.shape[2]
    sibling = (g, 2 * z + (1 - k))

    def z_peer(i):
        return lax.rem(z + i, chips)

    def g_peer(i):
        return lax.rem(g + i, groups)

    def copy(stage, slot, src, dst, device):
        return pltpu.make_async_remote_copy(
            src_ref=src, dst_ref=dst, send_sem=send[stage].at[slot], recv_sem=recv[stage].at[slot],
            device_id=device, device_id_type=MESH,
        )

    barrier = pltpu.get_barrier_semaphore()
    pl.semaphore_signal(barrier, inc=1, device_id=sibling, device_id_type=MESH)
    for i in range(1, chips):
        pl.semaphore_signal(barrier, inc=1, device_id=(g, 2 * z_peer(i) + k), device_id_type=MESH)
    for i in range(1, groups):
        pl.semaphore_signal(barrier, inc=1, device_id=(g_peer(i), c), device_id_type=MESH)

    own = pltpu.make_async_copy(a_ref, rows.at[pl.ds(64 * k, 64)], local.at[0])
    own.start()
    proj = fold3(dot(stack3(p_ref[...]), b_ref[...], NT), RANK)
    for kk in range(2):
        for zz in range(chips):
            halves[kk, zz] = proj[HALF * kk : HALF * (kk + 1), 128 * zz : 128 * (zz + 1)]
    pl.semaphore_wait(barrier, 1 + (chips - 1) + (groups - 1))

    send_half = copy("proj", 0, halves.at[1 - k], halves_in, sibling)
    send_half.start()
    send_rows = copy("rows", 0, a_ref, rows.at[pl.ds(64 * k, 64)], sibling)
    send_rows.start()
    send_half.wait_recv()

    psum[...] = halves[k] + halves_in[...]
    started = [send_half, send_rows]
    arriving = []
    for i in range(1, chips):
        to = z_peer(i)
        item = copy("zproj", i - 1, psum.at[to], psum_in.at[i - 1], (g, 2 * to + k))
        item.start()
        arriving.append(item)
    started += arriving
    mine = psum[z]
    for i, item in enumerate(arriving):
        item.wait_recv()
        mine = mine + psum_in[i]
    own.wait()
    send_rows.wait_recv()

    pieces = stack3(mine)
    arriving = []
    for i in range(1, groups + 1):
        to = lax.rem(g + i, groups)
        block = fold3(dot(pieces, rows[:, pl.ds(pl.multiple_of(wide * to, wide), wide)], NN), HALF)
        part[to] = block
        if i < groups:
            item = copy("xysum", i - 1, part.at[to], part_in.at[i - 1], (to, c))
            item.start()
            arriving.append(item)
    started += arriving
    mine = part[g]
    for i, item in enumerate(arriving):
        item.wait_recv()
        mine = mine + part_in[i]

    cols = wide // 128
    for j in range(chips):
        tile[j] = mine[8 * (j // cols) : 8 * (j // cols + 1), 128 * (j % cols) : 128 * (j % cols + 1)]
    arriving = []
    for i in range(1, chips):
        to = z_peer(i)
        item = copy("zsum", i - 1, tile.at[to], tile_in.at[i - 1], (g, 2 * to + k))
        item.start()
        arriving.append(item)
    started += arriving
    mine = tile[z]
    for i, item in enumerate(arriving):
        item.wait_recv()
        mine = mine + tile_in[i]
    tiles[z] = mine * (1.0 / groups)
    arriving = []
    for i in range(1, chips):
        item = copy("zgat", i - 1, tiles.at[z], tiles.at[z], (g, 2 * z_peer(i) + k))
        item.start()
        arriving.append(item)
    started += arriving
    for item in arriving:
        item.wait_recv()
    for j in range(chips):
        full[k, g, 8 * (j // cols) : 8 * (j // cols + 1), 128 * (j % cols) : 128 * (j % cols + 1)] = tiles[j]

    arriving = []
    for i in range(1, groups):
        item = copy("xygat", i - 1, full.at[k, g], full.at[k, g], (g_peer(i), c))
        item.start()
        arriving.append(item)
    started += arriving
    passed = [copy("half", 0, full.at[k, g], full.at[k, g], sibling)]
    passed[0].start()
    for i, item in enumerate(arriving):
        item.wait_recv()
        source = lax.rem(g + groups - (i + 1), groups)
        item = copy("half", i + 1, full.at[k, source], full.at[k, source], sibling)
        item.start()
        passed.append(item)
    started += passed
    for item in passed:
        item.wait_recv()

    gram = jnp.zeros((RANK, RANK), F32)
    for j in range(groups):
        block = jnp.concatenate([full[0, j], full[1, j]], axis=0)
        gram = gram + lax.dot_general(block, block, NT, precision=lax.Precision.HIGHEST, preferred_element_type=F32)
    inverse = inverse_factor(gram)
    q = jnp.zeros((3 * RANK, 128), F32)
    for j in range(groups):
        block = jnp.concatenate([full[0, j], full[1, j]], axis=0)
        block = lax.dot_general(inverse, block, NN, precision=lax.Precision.HIGHEST, preferred_element_type=F32)
        l_ref[:, wide * j : wide * (j + 1)] = block
        q = q + dot(stack3(block), rows[:, wide * j : wide * (j + 1)], NT)
    qs[z] = fold3(q, RANK)

    arriving = []
    for i in range(1, chips):
        item = copy("zq", i - 1, qs.at[z], qs.at[z], (g, 2 * z_peer(i) + k))
        item.start()
        arriving.append(item)
    started += arriving
    for item in arriving:
        item.wait_recv()
    q = jnp.concatenate([qs[j] for j in range(chips)], axis=1)
    factor = fold3(dot(stack3(q), b_ref[...], NN), RANK)

    tall = factor.shape[1] // 128
    for j in range(groups):
        if j < 2 * tall:
            fac[j] = factor[HALF * (j // tall) : HALF * (j // tall + 1), 128 * (j % tall) : 128 * (j % tall + 1)]
        else:
            fac[j] = jnp.zeros((HALF, 128), F32)
    arriving = []
    for i in range(1, groups):
        to = g_peer(i)
        item = copy("xyfac", i - 1, fac.at[to], fac_in.at[i - 1], (to, c))
        item.start()
        arriving.append(item)
    started += arriving
    mine = fac[g]
    for i, item in enumerate(arriving):
        item.wait_recv()
        mine = mine + fac_in[i]
    facs[g] = mine * (1.0 / groups)
    arriving = []
    for i in range(1, groups):
        item = copy("xyfacg", i - 1, facs.at[g], facs.at[g], (g_peer(i), c))
        item.start()
        arriving.append(item)
    started += arriving
    for item in arriving:
        item.wait_recv()
    for j in range(2 * tall):
        r_ref[HALF * (j // tall) : HALF * (j // tall + 1), 128 * (j % tall) : 128 * (j % tall + 1)] = facs[j]
    for item in started:
        item.wait_send()


def chain(groups, chips, rows, grads, prev):
    width, local = rows.shape[1], grads.shape[1]
    wide = width // groups
    counts = dict(
        rows=1, proj=1, zproj=chips - 1, xysum=groups - 1, zsum=chips - 1, zgat=chips - 1, xygat=groups - 1,
        half=groups, zq=chips - 1, xyfac=groups - 1, xyfacg=groups - 1,
    )
    dma = [pltpu.SemaphoreType.DMA((counts[s],)) for s in STAGES]
    vmem = pl.BlockSpec(memory_space=pltpu.VMEM)
    return pl.pallas_call(
        functools.partial(chain_kernel, groups, chips),
        out_shape=(jax.ShapeDtypeStruct((RANK, width), F32), jax.ShapeDtypeStruct((RANK, local), F32)),
        in_specs=[vmem] * 3,
        out_specs=(vmem, vmem),
        scratch_shapes=[
            pltpu.VMEM((128, width), BF16),
            pltpu.VMEM((2, chips, HALF, 128), F32),
            pltpu.VMEM((chips, HALF, 128), F32),
            pltpu.VMEM((chips, HALF, 128), F32),
            pltpu.VMEM((chips - 1, HALF, 128), F32),
            pltpu.VMEM((groups, HALF, wide), F32),
            pltpu.VMEM((groups - 1, HALF, wide), F32),
            pltpu.VMEM((chips, 8, 128), F32),
            pltpu.VMEM((chips - 1, 8, 128), F32),
            pltpu.VMEM((chips, 8, 128), F32),
            pltpu.VMEM((2, groups, HALF, wide), F32),
            pltpu.VMEM((chips, RANK, 128), F32),
            pltpu.VMEM((groups, HALF, 128), F32),
            pltpu.VMEM((groups - 1, HALF, 128), F32),
            pltpu.VMEM((groups, HALF, 128), F32),
            *dma,
            *dma,
            pltpu.SemaphoreType.DMA((1,)),
        ],
        compiler_params=pltpu.CompilerParams(collective_id=0, has_side_effects=True, vmem_limit_bytes=40 << 20),
        cost_estimate=pl.CostEstimate(flops=50_000_000_000, bytes_accessed=4 << 20, transcendentals=0),
        name="chain",
    )(rows, grads, prev)


def residual_kernel(a_ref, b_ref, l_ref, r_ref, out_ref, r3):
    @pl.when(pl.program_id(0) == 0)
    def _():
        hi, mid, _ = split3(r_ref[...])
        r3[0:RANK] = hi
        r3[RANK : 2 * RANK] = mid
        r3[2 * RANK :] = hi

    hi, mid, _ = split3(l_ref[...])
    left = jnp.concatenate([hi, hi, mid], axis=0)
    grad = dot(a_ref[...], b_ref[...], TN)
    out_ref[...] = (grad - dot(left, r3[...], TN)).astype(BF16)


def residual(gathered, grads, left, right, block=256):
    tokens, width = gathered.shape
    local = grads.shape[1]
    return pl.pallas_call(
        residual_kernel,
        grid=(width // block,),
        out_shape=jax.ShapeDtypeStruct((width, local), BF16),
        in_specs=[
            pl.BlockSpec((tokens, block), lambda i: (0, i)),
            pl.BlockSpec((tokens, local), lambda i: (0, 0)),
            pl.BlockSpec((RANK, block), lambda i: (0, i)),
            pl.BlockSpec((RANK, local), lambda i: (0, 0)),
        ],
        out_specs=pl.BlockSpec((block, local), lambda i: (i, 0)),
        scratch_shapes=[pltpu.VMEM((3 * RANK, local), BF16)],
        compiler_params=pltpu.CompilerParams(vmem_limit_bytes=58 << 20),
        name="residual",
    )(gathered, grads, left, right)


def body(groups, chips, activations, out_grads, prev_factor):
    rows, grads = activations[0], out_grads[0]
    gathered = lax.all_gather(rows, "col", axis=0, tiled=True)
    left, right = chain(groups, chips, rows, grads, prev_factor)
    return left, right, residual(gathered, grads, left, right)[None]


def solution(mesh):
    placed = (P("dp", "col", None), P("dp", None, "col"), P(None, "col"))
    return jax.shard_map(
        functools.partial(body, mesh.shape["dp"], mesh.shape["col"] // 2),
        mesh=mesh,
        in_specs=placed,
        out_specs=(P(), P(None, "col"), P("dp", None, "col")),
        check_vma=False,
    )
```

```python
import functools

import jax
import jax.numpy as jnp
from jax import lax
from jax.experimental import pallas as pl
from jax.experimental.pallas import tpu as pltpu
from jax.sharding import PartitionSpec as P

MESH = pl.DeviceIdType.MESH
F32 = jnp.float32
BF16 = jnp.bfloat16
RANK = 64
HALF = 32
STAGES = ("proj", "zproj", "xysum", "zsum", "zgat", "xygat", "half", "zq", "qhalf", "xyfac", "xyfacg")
CHUNK = 16


def split3(x):
    hi = x.astype(BF16)
    rest = x - hi.astype(F32)
    mid = rest.astype(BF16)
    lo = (rest - mid.astype(F32)).astype(BF16)
    return hi, mid, lo


def stack3(x):
    return jnp.concatenate(split3(x), axis=0)


def fold3(y, rows):
    return y[:rows] + (y[rows : 2 * rows] + y[2 * rows :])


NN = (((1,), (0,)), ((), ()))
NT = (((1,), (1,)), ((), ()))
TN = (((0,), (0,)), ((), ()))


def dot(a, b, dims):
    return lax.dot_general(a, b, dims, preferred_element_type=F32)


def inverse_factor(gram):
    n = gram.shape[0]
    row = lax.broadcasted_iota(jnp.int32, (n, n), 0)
    column = lax.broadcasted_iota(jnp.int32, (n, n), 1)
    work = jnp.concatenate([jnp.where(row == column, 1.0, 0.0).astype(F32), gram], axis=1)
    out = []
    for top in range(0, n, 8):
        shape = (n - top, 2 * n)
        for p in range(0, 8, 2):
            j = n + top + p
            c0 = jnp.broadcast_to(work[:, j : j + 1], shape)
            c1 = jnp.broadcast_to(work[:, j + 1 : j + 2], shape)
            a, b, d = c0[p : p + 1], c0[p + 1 : p + 2], c1[p + 1 : p + 2]
            over_a = 1.0 / a
            t = b * over_a
            s = d - b * t
            r0 = work[p : p + 1]
            r1 = work[p + 1 : p + 2] - t * r0
            out.append(r0 * lax.rsqrt(a))
            out.append(r1 * lax.rsqrt(s))
            if j + 2 < 2 * n:
                work = work - c0 * (r0 * over_a) - (c1 - c0 * t) * (r1 * (1.0 / s))
        work = work[8:]
    return jnp.concatenate(out, axis=0)[:, :n]


def offsets(chips):
    order = [0]
    for step in range(1, chips // 2):
        order += [chips - step, step]
    return order + [chips // 2]


def main_kernel(
    groups, chips, a_ref, b_ref, p_ref, l_ref, r_ref, grad_ref,
    acts, grads, prev, halves, halves_in, psum, psum_in, part, part_in, tile, tile_in, tiles, full, qs, fac, fac_in, facs,
    *sems,
):
    count = len(STAGES)
    send = dict(zip(STAGES, sems[:count]))
    recv = dict(zip(STAGES, sems[count : 2 * count]))
    ring_send, ring_recv, side_send, side_recv, local = sems[2 * count :]
    g = lax.axis_index("dp")
    c = lax.axis_index("col")
    z, k = c // 2, c % 2
    wide = part.shape[2]
    width = acts.shape[1]
    cols = wide // 128
    sibling = (g, 2 * z + (1 - k))
    order = offsets(chips)
    slot_of = {offset: slot for slot, offset in enumerate(order)}

    def chip(offset):
        return lax.rem(z + offset, chips)

    def peer(offset):
        return (g, 2 * chip(offset) + k)

    def group(offset):
        return lax.rem(g + offset, groups)

    def copy(stage, slot, src, dst, device):
        return pltpu.make_async_remote_copy(
            src_ref=src, dst_ref=dst, send_sem=send[stage].at[slot], recv_sem=recv[stage].at[slot],
            device_id=device, device_id_type=MESH,
        )

    started = []

    def begin(item):
        item.start()
        started.append(item)
        return item

    chunks = 64 // CHUNK
    last = chips // 2

    def chunk(slot, core, q):
        return acts.at[pl.ds(pl.multiple_of(128 * slot + 64 * core + CHUNK * q, CHUNK), CHUNK)]

    def ring(way, hop, q):
        offset = hop if way else chips - hop
        source = slot_of[(offset - (1 if way else -1)) % chips]
        return pltpu.make_async_remote_copy(
            src_ref=chunk(source, k, q), dst_ref=chunk(slot_of[offset % chips], k, q),
            send_sem=ring_send.at[way, hop - 1, q], recv_sem=ring_recv.at[way, hop - 1, q],
            device_id=peer(chips - 1 if way else 1), device_id_type=MESH,
        )

    steps = []
    for hop in range(1, last):
        steps += [[(0, hop, q), (1, hop, q)] for q in range(chunks)]
    steps += [[(0, last, q), (1, last, q + chunks // 2)] for q in range(chunks // 2)]
    final = {item for step in steps for item in step if item[1] == last}
    served = [0]
    side = []

    def pass_on(slot, q, rows=CHUNK):
        ref = acts.at[pl.ds(pl.multiple_of(128 * slot + 64 * k + CHUNK * q, CHUNK), rows)]
        n = len(side)
        side.append(begin(pltpu.make_async_remote_copy(
            src_ref=ref, dst_ref=ref, send_sem=side_send.at[n], recv_sem=side_recv.at[n],
            device_id=sibling, device_id_type=MESH,
        )))

    ringing = {}

    def serve(upto):
        for step in steps[served[0] : upto]:
            for way, hop, q in step:
                ringing[way, hop, q].wait_recv()
                after = (way, hop + 1, q)
                if hop + 1 < last or after in final:
                    ringing[after] = begin(ring(*after))
            for way, hop, q in step:
                pass_on(slot_of[(hop if way else chips - hop) % chips], q)
        served[0] = max(served[0], upto)

    side_done = [0]

    def side_wait(upto):
        for item in side[side_done[0] : 1 + 2 * upto]:
            item.wait_recv()
        side_done[0] = max(side_done[0], 1 + 2 * upto)

    def multiply(low, high):
        rows = slice(128 * low, 128 * high)
        block = min(1024, width)

        @pl.loop(0, width // block)
        def _(m):
            at = pl.ds(pl.multiple_of(m * block, block), block)
            value = dot(acts[rows, at], grads[rows, :], TN)
            grad_ref[at, :] = value if low == 0 else grad_ref[at, :] + value

    barrier = pltpu.get_barrier_semaphore()
    pl.semaphore_signal(barrier, inc=1, device_id=sibling, device_id_type=MESH)
    for i in range(1, chips):
        pl.semaphore_signal(barrier, inc=1, device_id=peer(i), device_id_type=MESH)
    for i in range(1, groups):
        pl.semaphore_signal(barrier, inc=1, device_id=(group(i), c), device_id_type=MESH)

    loads = [pltpu.make_async_copy(p_ref, prev, local.at[0])]
    for s in range(chips):
        at = pl.ds(pl.multiple_of(128 * chip(order[s]), 128), 128)
        loads.append(pltpu.make_async_copy(b_ref.at[at], grads.at[pl.ds(128 * s, 128)], local.at[1 + s]))
    own = pltpu.make_async_copy(a_ref, acts.at[pl.ds(pl.multiple_of(64 * k, 64), 64)], local.at[1 + chips])
    for item in loads:
        item.start()
    own.start()
    for item in loads:
        item.wait()
    proj = fold3(dot(stack3(prev[...]), grads[...], NT), RANK)
    for kk in range(2):
        for s in range(chips):
            halves[kk, s] = proj[HALF * kk : HALF * (kk + 1), 128 * s : 128 * (s + 1)]
    own.wait()
    pl.semaphore_wait(barrier, 1 + (chips - 1) + (groups - 1))

    send_half = begin(copy("proj", 0, halves.at[1 - k], halves_in, sibling))
    pass_on(0, 0, 64)
    if EARLY:
        for q in range(chunks):
            for way in range(2):
                ringing[way, 1, q] = begin(ring(way, 1, q))
    send_half.wait_recv()

    psum[...] = halves[k] + halves_in[...]
    arriving = [
        begin(copy("zproj", i - 1, psum.at[slot_of[i]], psum_in.at[i - 1], peer(i))) for i in range(1, chips)
    ]
    if not EARLY:
        for q in range(chunks):
            for way in range(2):
                ringing[way, 1, q] = begin(ring(way, 1, q))
    mine = psum[0]
    for i, item in enumerate(arriving):
        item.wait_recv()
        mine = mine + psum_in[i]
    side_wait(0)

    pieces = stack3(mine)
    arriving = []
    for i in range(1, groups + 1):
        to = group(i)
        part[to] = fold3(dot(pieces, acts[:128, pl.ds(pl.multiple_of(wide * to, wide), wide)], NN), HALF)
        if i < groups:
            arriving.append(begin(copy("xysum", i - 1, part.at[to], part_in.at[i - 1], (to, c))))
    serve(PLAN[0])
    mine = part[g]
    for i, item in enumerate(arriving):
        item.wait_recv()
        mine = mine + part_in[i]

    for j in range(chips):
        tile[j] = mine[8 * (j // cols) : 8 * (j // cols + 1), 128 * (j % cols) : 128 * (j % cols + 1)]
    arriving = [begin(copy("zsum", i - 1, tile.at[chip(i)], tile_in.at[i - 1], peer(i))) for i in range(1, chips)]
    serve(PLAN[1])
    mine = tile[z]
    for i, item in enumerate(arriving):
        item.wait_recv()
        mine = mine + tile_in[i]
    tiles[z] = mine * (1.0 / groups)
    arriving = [begin(copy("zgat", i - 1, tiles.at[z], tiles.at[z], peer(i))) for i in range(1, chips)]
    serve(PLAN[2])
    for item in arriving:
        item.wait_recv()
    for j in range(chips):
        full[k, g, 8 * (j // cols) : 8 * (j // cols + 1), 128 * (j % cols) : 128 * (j % cols + 1)] = tiles[j]

    arriving = [begin(copy("xygat", i - 1, full.at[k, g], full.at[k, g], (group(i), c))) for i in range(1, groups)]
    passed = []

    def meet(q, source):
        at = pl.ds(pl.multiple_of(wide * source, wide), wide)
        return q + dot(stack3(full[k, source]), acts[:128, at], NT)

    passed.append(begin(copy("half", 0, full.at[k, g], full.at[k, g], sibling)))
    q = meet(jnp.zeros((3 * HALF, 128), F32), g)
    serve(PLAN[3])
    for i, item in enumerate(arriving):
        item.wait_recv()
        source = group(groups - (i + 1))
        passed.append(begin(copy("half", i + 1, full.at[k, source], full.at[k, source], sibling)))
        q = meet(q, source)
    qs[k, 0] = fold3(q, HALF)

    arriving = [
        begin(copy("zq", i - 1, qs.at[k, 0], qs.at[k, slot_of[chips - i]], peer(i))) for i in range(1, chips)
    ]
    crossing = [begin(copy("qhalf", 0, qs.at[k, 0], qs.at[k, 0], sibling))]
    serve(PLAN[4])
    side_wait(served[0])
    multiply(0, chips // 2)
    serve(PLAN[5])
    for i, item in enumerate(arriving):
        item.wait_recv()
        here = qs.at[k, slot_of[chips - (i + 1)]]
        crossing.append(begin(copy("qhalf", i + 1, here, here, sibling)))
    for item in crossing:
        item.wait_recv()
    q = jnp.concatenate([jnp.concatenate([qs[0, s], qs[1, s]], axis=0) for s in range(chips)], axis=1)
    factor = fold3(dot(stack3(q), grads[...], NN), RANK)

    tall = factor.shape[1] // 128
    for j in range(groups):
        if j < 2 * tall:
            fac[j] = factor[HALF * (j // tall) : HALF * (j // tall + 1), 128 * (j % tall) : 128 * (j % tall + 1)]
        else:
            fac[j] = jnp.zeros((HALF, 128), F32)
    arriving = [
        begin(copy("xyfac", i - 1, fac.at[group(i)], fac_in.at[i - 1], (group(i), c))) for i in range(1, groups)
    ]
    serve(PLAN[6])
    for item in passed:
        item.wait_recv()
    gram = jnp.zeros((RANK, RANK), F32)
    for j in range(groups):
        block = jnp.concatenate([full[0, j], full[1, j]], axis=0)
        gram = gram + lax.dot_general(block, block, NT, precision=lax.Precision.HIGHEST, preferred_element_type=F32)
    inverse = inverse_factor(gram)
    serve(PLAN[7])
    mine = fac[g]
    for i, item in enumerate(arriving):
        item.wait_recv()
        mine = mine + fac_in[i]
    facs[g] = mine * (1.0 / groups)
    arriving = [begin(copy("xyfacg", i - 1, facs.at[g], facs.at[g], (group(i), c))) for i in range(1, groups)]
    serve(PLAN[8])
    for j in range(groups):
        block = jnp.concatenate([full[0, j], full[1, j]], axis=0)
        l_ref[:, wide * j : wide * (j + 1)] = lax.dot_general(
            inverse, block, NN, precision=lax.Precision.HIGHEST, preferred_element_type=F32
        )
    side_wait(served[0])
    multiply(chips // 2, 3 * chips // 4)
    serve(len(steps))
    side_wait(len(steps))
    multiply(3 * chips // 4, chips)
    for item in arriving:
        item.wait_recv()
    mean = jnp.concatenate(
        [jnp.concatenate([facs[tall * h + j] for j in range(tall)], axis=1) for h in range(2)], axis=0
    )
    r_ref[...] = lax.dot_general(inverse, mean, NN, precision=lax.Precision.HIGHEST, preferred_element_type=F32)
    for item in started:
        item.wait_send()


EARLY = False
PLAN = (3, 4, 6, 7, 9, 10, 11, 12, 13)


def low_rank(groups, chips, rows, grads, prev):
    width, local = rows.shape[1], grads.shape[1]
    wide = width // groups
    counts = dict(
        proj=1, zproj=chips - 1, xysum=groups - 1, zsum=chips - 1, zgat=chips - 1, xygat=groups - 1,
        half=groups, zq=chips - 1, qhalf=chips, xyfac=groups - 1, xyfacg=groups - 1,
    )
    dma = [pltpu.SemaphoreType.DMA((counts[s],)) for s in STAGES]
    chunks = 64 // CHUNK
    ring = pltpu.SemaphoreType.DMA((2, chips // 2, chunks))
    side = pltpu.SemaphoreType.DMA((1 + (chips - 1) * chunks,))
    hbm = pl.BlockSpec(memory_space=pl.ANY)
    vmem = pl.BlockSpec(memory_space=pltpu.VMEM)
    return pl.pallas_call(
        functools.partial(main_kernel, groups, chips),
        out_shape=(
            pltpu.VMEM((RANK, width), F32),
            pltpu.VMEM((RANK, local), F32),
            pltpu.VMEM((width, local), F32),
        ),
        in_specs=[hbm] * 3,
        out_specs=(vmem, vmem, vmem),
        scratch_shapes=[
            pltpu.VMEM((128 * chips, width), BF16),
            pltpu.VMEM((128 * chips, local), BF16),
            pltpu.VMEM((RANK, local), F32),
            pltpu.VMEM((2, chips, HALF, 128), F32),
            pltpu.VMEM((chips, HALF, 128), F32),
            pltpu.VMEM((chips, HALF, 128), F32),
            pltpu.VMEM((chips - 1, HALF, 128), F32),
            pltpu.VMEM((groups, HALF, wide), F32),
            pltpu.VMEM((groups - 1, HALF, wide), F32),
            pltpu.VMEM((chips, 8, 128), F32),
            pltpu.VMEM((chips - 1, 8, 128), F32),
            pltpu.VMEM((chips, 8, 128), F32),
            pltpu.VMEM((2, groups, HALF, wide), F32),
            pltpu.VMEM((2, chips, HALF, 128), F32),
            pltpu.VMEM((groups, HALF, 128), F32),
            pltpu.VMEM((groups - 1, HALF, 128), F32),
            pltpu.VMEM((groups, HALF, 128), F32),
            *dma,
            *dma,
            ring,
            ring,
            side,
            side,
            pltpu.SemaphoreType.DMA((2 + chips,)),
        ],
        compiler_params=pltpu.CompilerParams(collective_id=0, has_side_effects=True, vmem_limit_bytes=40 << 20),
        name="low_rank",
    )(rows, grads, prev)


def residual_kernel(grad_ref, l_ref, r_ref, l_out, r_out, out_ref, left, right, block, sems):
    out = [
        pltpu.make_async_copy(l_ref, l_out, sems.at[0]),
        pltpu.make_async_copy(r_ref, r_out, sems.at[1]),
    ]
    for item in out:
        item.start()
    hi, mid, _ = split3(l_ref[...])
    left[0:RANK] = hi
    left[RANK : 2 * RANK] = hi
    left[2 * RANK :] = mid
    hi, mid, _ = split3(r_ref[...])
    right[0:RANK] = hi
    right[RANK : 2 * RANK] = mid
    right[2 * RANK :] = hi
    slots, size = block.shape[:2]
    for m in range(grad_ref.shape[0] // size):
        at = slice(m * size, (m + 1) * size)
        if m >= slots:
            out[2 + m - slots].wait()
        block[m % slots] = (grad_ref[at] - dot(left[:, at], right[...], TN)).astype(BF16)
        item = pltpu.make_async_copy(block.at[m % slots], out_ref.at[at], sems.at[2 + m % slots])
        item.start()
        out.append(item)
    for item in out[:2] + out[-slots:]:
        item.wait()


def residual(grad, left, right):
    width, local = grad.shape
    size, slots = width // 8, 4
    hbm = pl.BlockSpec(memory_space=pl.ANY)
    vmem = pl.BlockSpec(memory_space=pltpu.VMEM)
    return pl.pallas_call(
        residual_kernel,
        out_shape=(
            jax.ShapeDtypeStruct(left.shape, F32),
            jax.ShapeDtypeStruct(right.shape, F32),
            jax.ShapeDtypeStruct((width, local), BF16),
        ),
        in_specs=[vmem] * 3,
        out_specs=(hbm, hbm, hbm),
        scratch_shapes=[
            pltpu.VMEM((3 * RANK, width), BF16),
            pltpu.VMEM((3 * RANK, local), BF16),
            pltpu.VMEM((slots, size, local), BF16),
            pltpu.SemaphoreType.DMA((2 + slots,)),
        ],
        compiler_params=pltpu.CompilerParams(vmem_limit_bytes=24 << 20),
        name="residual",
    )(grad, left, right)


def body(groups, chips, activations, out_grads, prev_factor):
    left, right, grad = low_rank(groups, chips, activations[0], out_grads[0], prev_factor)
    left, right, rest = residual(grad, left, right)
    return left, right, rest[None]


def solution(mesh):
    placed = (P("dp", "col", None), P("dp", None, "col"), P(None, "col"))
    return jax.shard_map(
        functools.partial(body, mesh.shape["dp"], mesh.shape["col"] // 2),
        mesh=mesh,
        in_specs=placed,
        out_specs=(P(), P(None, "col"), P("dp", None, "col")),
        check_vma=False,
    )
```

```python
import functools

import jax
import jax.numpy as jnp
from jax import lax
from jax.experimental import pallas as pl
from jax.experimental.pallas import tpu as pltpu
from jax.sharding import PartitionSpec as P

MESH = pl.DeviceIdType.MESH
F32 = jnp.float32
BF16 = jnp.bfloat16
RANK = 64
HALF = 32
STAGES = ("proj", "zproj", "xysum", "zsum", "zgat", "xygat", "half", "zq", "qhalf", "xyfac", "xyfacg")
CHUNK = 16


def split3(x):
    hi = x.astype(BF16)
    rest = x - hi.astype(F32)
    mid = rest.astype(BF16)
    lo = (rest - mid.astype(F32)).astype(BF16)
    return hi, mid, lo


def stack3(x):
    return jnp.concatenate(split3(x), axis=0)


def fold3(y, rows):
    return y[:rows] + (y[rows : 2 * rows] + y[2 * rows :])


NN = (((1,), (0,)), ((), ()))
NT = (((1,), (1,)), ((), ()))
TN = (((0,), (0,)), ((), ()))


def dot(a, b, dims):
    return lax.dot_general(a, b, dims, preferred_element_type=F32)


def inverse_factor(gram):
    n = gram.shape[0]
    row = lax.broadcasted_iota(jnp.int32, (n, n), 0)
    column = lax.broadcasted_iota(jnp.int32, (n, n), 1)
    work = jnp.concatenate([jnp.where(row == column, 1.0, 0.0).astype(F32), gram], axis=1)
    out = []
    for top in range(0, n, 8):
        shape = (n - top, 2 * n)
        for p in range(0, 8, 2):
            j = n + top + p
            c0 = jnp.broadcast_to(work[:, j : j + 1], shape)
            c1 = jnp.broadcast_to(work[:, j + 1 : j + 2], shape)
            a, b, d = c0[p : p + 1], c0[p + 1 : p + 2], c1[p + 1 : p + 2]
            over_a = 1.0 / a
            t = b * over_a
            s = d - b * t
            r0 = work[p : p + 1]
            r1 = work[p + 1 : p + 2] - t * r0
            out.append(r0 * lax.rsqrt(a))
            out.append(r1 * lax.rsqrt(s))
            if j + 2 < 2 * n:
                work = work - c0 * (r0 * over_a) - (c1 - c0 * t) * (r1 * (1.0 / s))
        work = work[8:]
    return jnp.concatenate(out, axis=0)[:, :n]


def offsets(chips):
    order = [0]
    for step in range(1, chips // 2):
        order += [chips - step, step]
    return order + [chips // 2]


def main_kernel(
    groups, chips, a_ref, b_ref, p_ref, l_ref, r_ref, grad_ref, late, late_grads,
    acts, grads, prev, halves, halves_in, psum, psum_in, part, part_in, tile, tile_in, tiles, full, qs, fac, fac_in, facs,
    *sems,
):
    count = len(STAGES)
    send = dict(zip(STAGES, sems[:count]))
    recv = dict(zip(STAGES, sems[count : 2 * count]))
    ring_send, ring_recv, side_send, side_recv, local = sems[2 * count :]
    g = lax.axis_index("dp")
    c = lax.axis_index("col")
    z, k = c // 2, c % 2
    wide = part.shape[2]
    width = acts.shape[1]
    cols = wide // 128
    sibling = (g, 2 * z + (1 - k))
    order = offsets(chips)
    slot_of = {offset: slot for slot, offset in enumerate(order)}

    def chip(offset):
        return lax.rem(z + offset, chips)

    def peer(offset):
        return (g, 2 * chip(offset) + k)

    def group(offset):
        return lax.rem(g + offset, groups)

    def copy(stage, slot, src, dst, device):
        return pltpu.make_async_remote_copy(
            src_ref=src, dst_ref=dst, send_sem=send[stage].at[slot], recv_sem=recv[stage].at[slot],
            device_id=device, device_id_type=MESH,
        )

    started = []

    def begin(item):
        item.start()
        started.append(item)
        return item

    def drain(all_of_them=False):
        keep = 0 if all_of_them else 3 * groups
        done = started[: max(0, len(started) - keep)]
        for item in done:
            item.wait_send()
        del started[: len(done)]

    chunks = 64 // CHUNK
    last = chips // 2

    def chunk(slot, core, q, rows=CHUNK):
        early = acts.shape[0] // 128
        ref, slot = (acts, slot) if slot < early else (late, slot - early)
        return ref.at[pl.ds(pl.multiple_of(128 * slot + 64 * core + CHUNK * q, CHUNK), rows)]

    def ring(way, hop, q):
        offset = hop if way else chips - hop
        source = slot_of[(offset - (1 if way else -1)) % chips]
        return pltpu.make_async_remote_copy(
            src_ref=chunk(source, k, q), dst_ref=chunk(slot_of[offset % chips], k, q),
            send_sem=ring_send.at[way, hop - 1, q], recv_sem=ring_recv.at[way, hop - 1, q],
            device_id=peer(chips - 1 if way else 1), device_id_type=MESH,
        )

    steps = []
    for hop in range(1, last):
        steps += [[(0, hop, q), (1, hop, q)] for q in range(chunks)]
    steps += [[(0, last, q), (1, last, q + chunks // 2)] for q in range(chunks // 2)]
    final = {item for step in steps for item in step if item[1] == last}
    served = [0]
    side = []

    def pass_on(slot, q, rows=CHUNK):
        ref = chunk(slot, k, q, rows)
        n = len(side)
        side.append(begin(pltpu.make_async_remote_copy(
            src_ref=ref, dst_ref=ref, send_sem=side_send.at[n], recv_sem=side_recv.at[n],
            device_id=sibling, device_id_type=MESH,
        )))

    ringing = {}

    def serve(upto):
        for step in steps[served[0] : upto]:
            for way, hop, q in step:
                ringing[way, hop, q].wait_recv()
                after = (way, hop + 1, q)
                if hop + 1 < last or after in final:
                    ringing[after] = begin(ring(*after))
            for way, hop, q in step:
                pass_on(slot_of[(hop if way else chips - hop) % chips], q)
        served[0] = max(served[0], upto)

    side_done = [0]

    def side_wait(upto):
        for item in side[side_done[0] : 1 + 2 * upto]:
            item.wait_recv()
        side_done[0] = max(side_done[0], 1 + 2 * upto)

    def multiply(low, high):
        rows = slice(128 * low, 128 * high)
        block = min(1024, width)

        @pl.loop(0, width // block)
        def _(m):
            at = pl.ds(pl.multiple_of(m * block, block), block)
            value = dot(acts[rows, at], grads[rows, :], TN)
            grad_ref[at, :] = value if low == 0 else grad_ref[at, :] + value

    barrier = pltpu.get_barrier_semaphore()
    pl.semaphore_signal(barrier, inc=1, device_id=sibling, device_id_type=MESH)
    for i in range(1, chips):
        pl.semaphore_signal(barrier, inc=1, device_id=peer(i), device_id_type=MESH)
    for i in range(1, groups):
        pl.semaphore_signal(barrier, inc=1, device_id=(group(i), c), device_id_type=MESH)

    loads = [pltpu.make_async_copy(p_ref, prev, local.at[0])]
    for s in range(chips):
        at = pl.ds(pl.multiple_of(128 * chip(order[s]), 128), 128)
        loads.append(pltpu.make_async_copy(b_ref.at[at], grads.at[pl.ds(128 * s, 128)], local.at[1 + s]))
    own = pltpu.make_async_copy(a_ref, acts.at[pl.ds(pl.multiple_of(64 * k, 64), 64)], local.at[1 + chips])
    for item in loads:
        item.start()
    own.start()
    for item in loads:
        item.wait()
    late_grads[...] = grads[96 * chips :]
    proj = fold3(dot(stack3(prev[...]), grads[...], NT), RANK)
    for kk in range(2):
        for s in range(chips):
            halves[kk, s] = proj[HALF * kk : HALF * (kk + 1), 128 * s : 128 * (s + 1)]
    own.wait()
    pl.semaphore_wait(barrier, 1 + (chips - 1) + (groups - 1))

    send_half = begin(copy("proj", 0, halves.at[1 - k], halves_in, sibling))
    pass_on(0, 0, 64)
    for way in range(2):
        ringing[way, 1, 0] = begin(ring(way, 1, 0))
    send_half.wait_recv()

    psum[...] = halves[k] + halves_in[...]
    arriving = [
        begin(copy("zproj", i - 1, psum.at[slot_of[i]], psum_in.at[i - 1], peer(i))) for i in range(1, chips)
    ]
    for q in range(1, chunks):
        for way in range(2):
            ringing[way, 1, q] = begin(ring(way, 1, q))
    mine = psum[0]
    for i, item in enumerate(arriving):
        item.wait_recv()
        mine = mine + psum_in[i]
    side_wait(0)

    pieces = stack3(mine)
    arriving = []
    for first in range(1, groups + 1, 4):
        batch = range(first, first + 4)
        blocks = [
            fold3(dot(pieces, acts[:128, pl.ds(pl.multiple_of(wide * group(i), wide), wide)], NN), HALF) for i in batch
        ]
        for i, block in zip(batch, blocks):
            part[group(i)] = block
        for i in batch:
            if i < groups:
                arriving.append(
                    begin(copy("xysum", i - 1, part.at[group(i)], part_in.at[i - 1], (group(i), c)))
                )
    serve(PLAN[0])
    mine = part[g]
    for i, item in enumerate(arriving):
        item.wait_recv()
        mine = mine + part_in[i]

    for j in range(chips):
        tile[j] = mine[8 * (j // cols) : 8 * (j // cols + 1), 128 * (j % cols) : 128 * (j % cols + 1)]
    arriving = [begin(copy("zsum", i - 1, tile.at[chip(i)], tile_in.at[i - 1], peer(i))) for i in range(1, chips)]
    serve(PLAN[1])
    mine = tile[z]
    for i, item in enumerate(arriving):
        item.wait_recv()
        mine = mine + tile_in[i]
    tiles[z] = mine * (1.0 / groups)
    arriving = [begin(copy("zgat", i - 1, tiles.at[z], tiles.at[z], peer(i))) for i in range(1, chips)]
    serve(PLAN[2])
    for item in arriving:
        item.wait_recv()
    for j in range(chips):
        full[k, g, 8 * (j // cols) : 8 * (j // cols + 1), 128 * (j % cols) : 128 * (j % cols + 1)] = tiles[j]

    arriving = [begin(copy("xygat", i - 1, full.at[k, g], full.at[k, g], (group(i), c))) for i in range(1, groups)]
    passed = []

    def meet(source):
        at = pl.ds(pl.multiple_of(wide * source, wide), wide)
        return dot(stack3(full[k, source]), acts[:128, at], NT)

    passed.append(begin(copy("half", 0, full.at[k, g], full.at[k, g], sibling)))
    q = meet(g)
    serve(PLAN[3])
    for first in range(0, groups - 1, 4):
        batch = range(first, min(first + 4, groups - 1))
        if first == groups // 2:
            serve(PLAN[4])
        sources = [group(groups - (i + 1)) for i in batch]
        for i, source in zip(batch, sources):
            arriving[i].wait_recv()
            passed.append(begin(copy("half", i + 1, full.at[k, source], full.at[k, source], sibling)))
        for source in sources:
            q = q + meet(source)
    qs[k, 0] = fold3(q, HALF)

    arriving = [
        begin(copy("zq", i - 1, qs.at[k, 0], qs.at[k, slot_of[chips - i]], peer(i))) for i in range(1, chips)
    ]
    crossing = [begin(copy("qhalf", 0, qs.at[k, 0], qs.at[k, 0], sibling))]
    serve(PLAN[5])
    for item in passed:
        item.wait_recv()
    gram = jnp.zeros((RANK, RANK), F32)
    for j in range(groups):
        block = jnp.concatenate([full[0, j], full[1, j]], axis=0)
        gram = gram + lax.dot_general(block, block, NT, precision=lax.Precision.HIGHEST, preferred_element_type=F32)
    inverse = inverse_factor(gram)
    serve(PLAN[6])
    for i, item in enumerate(arriving):
        item.wait_recv()
        here = qs.at[k, slot_of[chips - (i + 1)]]
        crossing.append(begin(copy("qhalf", i + 1, here, here, sibling)))
    for item in crossing:
        item.wait_recv()
    q = jnp.concatenate([jnp.concatenate([qs[0, s], qs[1, s]], axis=0) for s in range(chips)], axis=1)
    factor = fold3(dot(stack3(q), grads[...], NN), RANK)

    tall = factor.shape[1] // 128
    for j in range(groups):
        if j < 2 * tall:
            fac[j] = factor[HALF * (j // tall) : HALF * (j // tall + 1), 128 * (j % tall) : 128 * (j % tall + 1)]
        else:
            fac[j] = jnp.zeros((HALF, 128), F32)
    arriving = [
        begin(copy("xyfac", i - 1, fac.at[group(i)], fac_in.at[i - 1], (group(i), c))) for i in range(1, groups)
    ]
    serve(PLAN[7])
    side_wait(served[0])
    multiply(0, chips // 2)
    drain()
    serve(PLAN[8])
    mine = fac[g]
    for i, item in enumerate(arriving):
        item.wait_recv()
        mine = mine + fac_in[i]
    facs[g] = mine * (1.0 / groups)
    arriving = [begin(copy("xyfacg", i - 1, facs.at[g], facs.at[g], (group(i), c))) for i in range(1, groups)]
    serve(PLAN[9])
    for j in range(groups):
        block = jnp.concatenate([full[0, j], full[1, j]], axis=0)
        l_ref[:, wide * j : wide * (j + 1)] = lax.dot_general(
            inverse, block, NN, precision=lax.Precision.HIGHEST, preferred_element_type=F32
        )
    side_wait(served[0])
    multiply(chips // 2, 3 * chips // 4)
    drain()
    for item in arriving:
        item.wait_recv()
    mean = jnp.concatenate(
        [jnp.concatenate([facs[tall * h + j] for j in range(tall)], axis=1) for h in range(2)], axis=0
    )
    r_ref[...] = lax.dot_general(inverse, mean, NN, precision=lax.Precision.HIGHEST, preferred_element_type=F32)
    serve(len(steps))
    side_wait(len(steps))
    drain(True)


PLAN = (1, 2, 3, 4, 5, 6, 8, 8, 10, 12)


def low_rank(groups, chips, rows, grads, prev):
    width, local = rows.shape[1], grads.shape[1]
    wide = width // groups
    counts = dict(
        proj=1, zproj=chips - 1, xysum=groups - 1, zsum=chips - 1, zgat=chips - 1, xygat=groups - 1,
        half=groups, zq=chips - 1, qhalf=chips, xyfac=groups - 1, xyfacg=groups - 1,
    )
    dma = [pltpu.SemaphoreType.DMA((counts[s],)) for s in STAGES]
    chunks = 64 // CHUNK
    ring = pltpu.SemaphoreType.DMA((2, chips // 2, chunks))
    side = pltpu.SemaphoreType.DMA((1 + (chips - 1) * chunks,))
    hbm = pl.BlockSpec(memory_space=pl.ANY)
    vmem = pl.BlockSpec(memory_space=pltpu.VMEM)
    return pl.pallas_call(
        functools.partial(main_kernel, groups, chips),
        out_shape=(
            pltpu.VMEM((RANK, width), F32),
            pltpu.VMEM((RANK, local), F32),
            pltpu.VMEM((width, local), F32),
            pltpu.VMEM((32 * chips, width), BF16),
            pltpu.VMEM((32 * chips, local), BF16),
        ),
        in_specs=[hbm] * 3,
        out_specs=(vmem,) * 5,
        scratch_shapes=[
            pltpu.VMEM((96 * chips, width), BF16),
            pltpu.VMEM((128 * chips, local), BF16),
            pltpu.VMEM((RANK, local), F32),
            pltpu.VMEM((2, chips, HALF, 128), F32),
            pltpu.VMEM((chips, HALF, 128), F32),
            pltpu.VMEM((chips, HALF, 128), F32),
            pltpu.VMEM((chips - 1, HALF, 128), F32),
            pltpu.VMEM((groups, HALF, wide), F32),
            pltpu.VMEM((groups - 1, HALF, wide), F32),
            pltpu.VMEM((chips, 8, 128), F32),
            pltpu.VMEM((chips - 1, 8, 128), F32),
            pltpu.VMEM((chips, 8, 128), F32),
            pltpu.VMEM((2, groups, HALF, wide), F32),
            pltpu.VMEM((2, chips, HALF, 128), F32),
            pltpu.VMEM((groups, HALF, 128), F32),
            pltpu.VMEM((groups - 1, HALF, 128), F32),
            pltpu.VMEM((groups, HALF, 128), F32),
            *dma,
            *dma,
            ring,
            ring,
            side,
            side,
            pltpu.SemaphoreType.DMA((2 + chips,)),
        ],
        compiler_params=pltpu.CompilerParams(collective_id=0, has_side_effects=True, vmem_limit_bytes=37 << 20),
        name="low_rank",
    )(rows, grads, prev)


def residual_kernel(grad_ref, late, late_grads, l_ref, r_ref, l_out, r_out, out_ref, left, right, block, sems):
    out = [
        pltpu.make_async_copy(l_ref, l_out, sems.at[0]),
        pltpu.make_async_copy(r_ref, r_out, sems.at[1]),
    ]
    for item in out:
        item.start()
    hi, mid, _ = split3(l_ref[...])
    left[0:RANK] = hi
    left[RANK : 2 * RANK] = hi
    left[2 * RANK :] = mid
    hi, mid, _ = split3(r_ref[...])
    right[0:RANK] = hi
    right[RANK : 2 * RANK] = mid
    right[2 * RANK :] = hi
    slots, size = block.shape[:2]
    for m in range(grad_ref.shape[0] // size):
        at = slice(m * size, (m + 1) * size)
        if m >= slots:
            out[2 + m - slots].wait()
        rest = dot(late[:, at], late_grads[...], TN) - dot(left[:, at], right[...], TN)
        block[m % slots] = (grad_ref[at] + rest).astype(BF16)
        item = pltpu.make_async_copy(block.at[m % slots], out_ref.at[at], sems.at[2 + m % slots])
        item.start()
        out.append(item)
    for item in out[:2] + out[-slots:]:
        item.wait()


def residual(grad, late, late_grads, left, right):
    width, local = grad.shape
    size, slots = width // 8, 4
    hbm = pl.BlockSpec(memory_space=pl.ANY)
    vmem = pl.BlockSpec(memory_space=pltpu.VMEM)
    return pl.pallas_call(
        residual_kernel,
        out_shape=(
            jax.ShapeDtypeStruct(left.shape, F32),
            jax.ShapeDtypeStruct(right.shape, F32),
            jax.ShapeDtypeStruct((width, local), BF16),
        ),
        in_specs=[vmem] * 5,
        out_specs=(hbm, hbm, hbm),
        scratch_shapes=[
            pltpu.VMEM((3 * RANK, width), BF16),
            pltpu.VMEM((3 * RANK, local), BF16),
            pltpu.VMEM((slots, size, local), BF16),
            pltpu.SemaphoreType.DMA((2 + slots,)),
        ],
        compiler_params=pltpu.CompilerParams(vmem_limit_bytes=16 << 20),
        name="residual",
    )(grad, late, late_grads, left, right)


def body(groups, chips, activations, out_grads, prev_factor):
    left, right, *parts = low_rank(groups, chips, activations[0], out_grads[0], prev_factor)
    left, right, rest = residual(*parts, left, right)
    return left, right, rest[None]


def solution(mesh):
    placed = (P("dp", "col", None), P("dp", None, "col"), P(None, "col"))
    return jax.shard_map(
        functools.partial(body, mesh.shape["dp"], mesh.shape["col"] // 2),
        mesh=mesh,
        in_specs=placed,
        out_specs=(P(), P(None, "col"), P("dp", None, "col")),
        check_vma=False,
    )
```

```python
import functools
import math

import jax
import jax.numpy as jnp
from jax import lax
from jax.experimental import pallas as pl
from jax.experimental.pallas import tpu as pltpu
from jax.sharding import PartitionSpec as P

MESH = pl.DeviceIdType.MESH
F32 = jnp.float32
BF16 = jnp.bfloat16
RANK = 64
HALF = 32
STAGES = ("proj", "zproj", "xysum", "zsum", "zgat", "xygat", "half", "zq", "qhalf", "xyfac", "xyfacg")
CHUNK = 16


def split3(x):
    hi = x.astype(BF16)
    rest = x - hi.astype(F32)
    mid = rest.astype(BF16)
    lo = (rest - mid.astype(F32)).astype(BF16)
    return hi, mid, lo


def stack3(x):
    return jnp.concatenate(split3(x), axis=0)


def fold3(y, rows):
    return y[:rows] + (y[rows : 2 * rows] + y[2 * rows :])


NN = (((1,), (0,)), ((), ()))
NT = (((1,), (1,)), ((), ()))
TN = (((0,), (0,)), ((), ()))


def dot(a, b, dims):
    return lax.dot_general(a, b, dims, preferred_element_type=F32)


def inverse_factor(gram):
    n = gram.shape[0]
    row = lax.broadcasted_iota(jnp.int32, (n, n), 0)
    column = lax.broadcasted_iota(jnp.int32, (n, n), 1)
    work = jnp.concatenate([jnp.where(row == column, 1.0, 0.0).astype(F32), gram], axis=1)
    out = []
    for top in range(0, n, 8):
        shape = (n - top, 2 * n)
        for p in range(0, 8, 2):
            j = n + top + p
            c0 = jnp.broadcast_to(work[:, j : j + 1], shape)
            c1 = jnp.broadcast_to(work[:, j + 1 : j + 2], shape)
            a, b, d = c0[p : p + 1], c0[p + 1 : p + 2], c1[p + 1 : p + 2]
            over_a = 1.0 / a
            t = b * over_a
            s = d - b * t
            r0 = work[p : p + 1]
            r1 = work[p + 1 : p + 2] - t * r0
            out.append(r0 * lax.rsqrt(a))
            out.append(r1 * lax.rsqrt(s))
            if j + 2 < 2 * n:
                work = work - c0 * (r0 * over_a) - (c1 - c0 * t) * (r1 * (1.0 / s))
        work = work[8:]
    return jnp.concatenate(out, axis=0)[:, :n]


def offsets(chips):
    order = [0]
    for step in range(1, chips // 2):
        order += [chips - step, step]
    return order + [chips // 2]


def main_kernel(
    groups, chips, a_ref, b_ref, p_ref, l_ref, r_ref, left, right, grad_ref, late, late_grads,
    acts, grads, prev, halves, halves_in, psum, psum_in, part, part_in, tile, tile_in, tiles, full, qs, fac, fac_in, facs,
    *sems,
):
    count = len(STAGES)
    send = dict(zip(STAGES, sems[:count]))
    recv = dict(zip(STAGES, sems[count : 2 * count]))
    ring_send, ring_recv, side_send, side_recv, local = sems[2 * count :]
    g = lax.axis_index("dp")
    c = lax.axis_index("col")
    z, k = c // 2, c % 2
    wide = part.shape[2]
    width = acts.shape[1]
    cols = wide // 128
    sibling = (g, 2 * z + (1 - k))
    order = offsets(chips)
    slot_of = {offset: slot for slot, offset in enumerate(order)}

    def chip(offset):
        return lax.rem(z + offset, chips)

    def peer(offset):
        return (g, 2 * chip(offset) + k)

    edge = math.isqrt(groups)
    moves = [(dx, dy) for dx in range(edge) for dy in range(edge)]
    moves.sort(key=lambda move: -sum(min(d, edge - d) for d in move))
    far_first = sorted(range(1, chips), key=lambda i: -min(i, chips - i))

    def group(i, sign=1):
        dx, dy = moves[i - 1]
        x, y = lax.rem(g // edge + sign * dx + edge, edge), lax.rem(lax.rem(g, edge) + sign * dy + edge, edge)
        return x * edge + y

    def copy(stage, slot, src, dst, device):
        return pltpu.make_async_remote_copy(
            src_ref=src, dst_ref=dst, send_sem=send[stage].at[slot], recv_sem=recv[stage].at[slot],
            device_id=device, device_id_type=MESH,
        )

    started = []

    def begin(item):
        item.start()
        started.append(item)
        return item

    def drain(all_of_them=False):
        keep = 0 if all_of_them else 2 * groups
        done = started[: max(0, len(started) - keep)]
        for item in done:
            item.wait_send()
        del started[: len(done)]

    chunks = 64 // CHUNK
    last = chips // 2

    def chunk(slot, core, q, rows=CHUNK):
        early = acts.shape[0] // 128
        ref, slot = (acts, slot) if slot < early else (late, slot - early)
        return ref.at[pl.ds(pl.multiple_of(128 * slot + 64 * core + CHUNK * q, CHUNK), rows)]

    def ring(way, hop, q):
        offset = hop if way else chips - hop
        source = slot_of[(offset - (1 if way else -1)) % chips]
        return pltpu.make_async_remote_copy(
            src_ref=chunk(source, k, q), dst_ref=chunk(slot_of[offset % chips], k, q),
            send_sem=ring_send.at[way, hop - 1, q], recv_sem=ring_recv.at[way, hop - 1, q],
            device_id=peer(chips - 1 if way else 1), device_id_type=MESH,
        )

    steps = []
    for hop in range(1, last):
        steps += [[(0, hop, q), (1, hop, q)] for q in range(chunks)]
    steps += [[(0, last, q), (1, last, q + chunks // 2)] for q in range(chunks // 2)]
    final = {item for step in steps for item in step if item[1] == last}
    served = [0]
    side = []

    def pass_on(slot, q, rows=CHUNK):
        ref = chunk(slot, k, q, rows)
        n = len(side)
        side.append(begin(pltpu.make_async_remote_copy(
            src_ref=ref, dst_ref=ref, send_sem=side_send.at[n], recv_sem=side_recv.at[n],
            device_id=sibling, device_id_type=MESH,
        )))

    ringing = {}

    def serve(upto):
        for step in steps[served[0] : upto]:
            for way, hop, q in step:
                ringing[way, hop, q].wait_recv()
                after = (way, hop + 1, q)
                if hop + 1 < last or after in final:
                    ringing[after] = begin(ring(*after))
            for way, hop, q in step:
                pass_on(slot_of[(hop if way else chips - hop) % chips], q)
        served[0] = max(served[0], upto)

    side_done = [0]

    def side_wait(upto):
        for item in side[side_done[0] : 1 + 2 * upto]:
            item.wait_recv()
        side_done[0] = max(side_done[0], 1 + 2 * upto)

    def multiply(low, high):
        rows = slice(128 * low, 128 * high)
        block = min(1024, width)

        @pl.loop(0, width // block)
        def _(m):
            at = pl.ds(pl.multiple_of(m * block, block), block)
            value = dot(acts[rows, at], grads[rows, :], TN)
            grad_ref[at, :] = value if low == 0 else grad_ref[at, :] + value

    barrier = pltpu.get_barrier_semaphore()
    pl.semaphore_signal(barrier, inc=1, device_id=sibling, device_id_type=MESH)
    for i in range(1, chips):
        pl.semaphore_signal(barrier, inc=1, device_id=peer(i), device_id_type=MESH)
    for i in range(1, groups):
        pl.semaphore_signal(barrier, inc=1, device_id=(group(i), c), device_id_type=MESH)

    loads = [pltpu.make_async_copy(p_ref, prev, local.at[0])]
    for s in range(chips):
        at = pl.ds(pl.multiple_of(128 * chip(order[s]), 128), 128)
        loads.append(pltpu.make_async_copy(b_ref.at[at], grads.at[pl.ds(128 * s, 128)], local.at[1 + s]))
    own = pltpu.make_async_copy(a_ref, acts.at[pl.ds(pl.multiple_of(64 * k, 64), 64)], local.at[1 + chips])
    for item in loads:
        item.start()
    own.start()
    for item in loads:
        item.wait()
    late_grads[...] = grads[96 * chips :]
    proj = fold3(dot(stack3(prev[...]), grads[...], NT), RANK)
    for kk in range(2):
        for s in range(chips):
            halves[kk, s] = proj[HALF * kk : HALF * (kk + 1), 128 * s : 128 * (s + 1)]
    own.wait()
    pl.semaphore_wait(barrier, 1 + (chips - 1) + (groups - 1))

    send_half = begin(copy("proj", 0, halves.at[1 - k], halves_in, sibling))
    pass_on(0, 0, 64)
    for way in range(2):
        ringing[way, 1, 0] = begin(ring(way, 1, 0))
    send_half.wait_recv()

    psum[...] = halves[k] + halves_in[...]
    arriving = [
        begin(copy("zproj", i - 1, psum.at[slot_of[i]], psum_in.at[i - 1], peer(i))) for i in far_first
    ]
    for q in range(1, chunks):
        for way in range(2):
            ringing[way, 1, q] = begin(ring(way, 1, q))
    mine = psum[0]
    for i, item in zip(far_first[::-1], arriving[::-1]):
        item.wait_recv()
        mine = mine + psum_in[i - 1]
    side_wait(0)

    pieces = stack3(mine)
    arriving = []
    for first in range(1, groups + 1, 4):
        batch = range(first, first + 4)
        blocks = [
            fold3(dot(pieces, acts[:128, pl.ds(pl.multiple_of(wide * group(i), wide), wide)], NN), HALF) for i in batch
        ]
        for i, block in zip(batch, blocks):
            part[group(i)] = block
        for i in batch:
            if i < groups:
                arriving.append(
                    begin(copy("xysum", i - 1, part.at[group(i)], part_in.at[i - 1], (group(i), c)))
                )
    serve(PLAN[0])
    mine = part[g]
    for i, item in enumerate(arriving):
        item.wait_recv()
        mine = mine + part_in[i]

    for j in range(chips):
        tile[j] = mine[8 * (j // cols) : 8 * (j // cols + 1), 128 * (j % cols) : 128 * (j % cols + 1)]
    arriving = [begin(copy("zsum", i - 1, tile.at[chip(i)], tile_in.at[i - 1], peer(i))) for i in far_first]
    serve(PLAN[1])
    mine = tile[z]
    for i, item in zip(far_first[::-1], arriving[::-1]):
        item.wait_recv()
        mine = mine + tile_in[i - 1]
    tiles[z] = mine * (1.0 / groups)
    arriving = [begin(copy("zgat", i - 1, tiles.at[z], tiles.at[z], peer(i))) for i in far_first]
    serve(PLAN[2])
    for item in arriving:
        item.wait_recv()
    for j in range(chips):
        full[k, g, 8 * (j // cols) : 8 * (j // cols + 1), 128 * (j % cols) : 128 * (j % cols + 1)] = tiles[j]

    arriving = [begin(copy("xygat", i - 1, full.at[k, g], full.at[k, g], (group(i), c))) for i in range(1, groups)]
    passed = []

    def meet(source):
        at = pl.ds(pl.multiple_of(wide * source, wide), wide)
        return dot(stack3(full[k, source]), acts[:128, at], NT)

    passed.append(begin(copy("half", 0, full.at[k, g], full.at[k, g], sibling)))
    q = meet(g)
    serve(PLAN[3])
    near_first = list(range(groups - 1))[::-1]
    for first in range(0, groups - 1, 4):
        batch = near_first[first : first + 4]
        if first == groups // 2:
            serve(PLAN[4])
        sources = [group(i + 1, -1) for i in batch]
        for i, source in zip(batch, sources):
            arriving[i].wait_recv()
            passed.append(begin(copy("half", i + 1, full.at[k, source], full.at[k, source], sibling)))
        for source in sources:
            q = q + meet(source)
    qs[k, 0] = fold3(q, HALF)

    arriving = [
        begin(copy("zq", i - 1, qs.at[k, 0], qs.at[k, slot_of[chips - i]], peer(i))) for i in far_first
    ]
    crossing = [begin(copy("qhalf", 0, qs.at[k, 0], qs.at[k, 0], sibling))]
    serve(PLAN[5])
    for item in passed:
        item.wait_recv()
    gram = jnp.zeros((RANK, RANK), F32)
    for j in range(groups):
        block = jnp.concatenate([full[0, j], full[1, j]], axis=0)
        gram = gram + lax.dot_general(block, block, NT, precision=lax.Precision.HIGHEST, preferred_element_type=F32)
    inverse = inverse_factor(gram)
    serve(PLAN[6])
    for i, item in zip(far_first[::-1], arriving[::-1]):
        item.wait_recv()
        here = qs.at[k, slot_of[chips - i]]
        crossing.append(begin(copy("qhalf", i, here, here, sibling)))
    for item in crossing:
        item.wait_recv()
    q = jnp.concatenate([jnp.concatenate([qs[0, s], qs[1, s]], axis=0) for s in range(chips)], axis=1)
    factor = fold3(dot(stack3(q), grads[...], NN), RANK)

    tall = factor.shape[1] // 128
    for j in range(groups):
        if j < 2 * tall:
            fac[j] = factor[HALF * (j // tall) : HALF * (j // tall + 1), 128 * (j % tall) : 128 * (j % tall + 1)]
        else:
            fac[j] = jnp.zeros((HALF, 128), F32)
    arriving = [
        begin(copy("xyfac", i - 1, fac.at[group(i)], fac_in.at[i - 1], (group(i), c))) for i in range(1, groups)
    ]
    serve(PLAN[7])
    side_wait(served[0])
    multiply(0, chips // 2)
    drain()
    serve(PLAN[8])
    mine = fac[g]
    for i, item in enumerate(arriving):
        item.wait_recv()
        mine = mine + fac_in[i]
    facs[g] = mine * (1.0 / groups)
    arriving = [begin(copy("xyfacg", i - 1, facs.at[g], facs.at[g], (group(i), c))) for i in range(1, groups)]
    serve(PLAN[9])
    for j in range(groups):
        block = jnp.concatenate([full[0, j], full[1, j]], axis=0)
        at = slice(wide * j, wide * (j + 1))
        block = lax.dot_general(inverse, block, NN, precision=lax.Precision.HIGHEST, preferred_element_type=F32)
        l_ref[:, at] = block
        hi, mid, _ = split3(block)
        left[:, at] = jnp.concatenate([hi, hi, mid], axis=0)
    side_wait(served[0])
    multiply(chips // 2, 3 * chips // 4)
    drain()
    for item in arriving:
        item.wait_recv()
    mean = jnp.concatenate(
        [jnp.concatenate([facs[tall * h + j] for j in range(tall)], axis=1) for h in range(2)], axis=0
    )
    mean = lax.dot_general(inverse, mean, NN, precision=lax.Precision.HIGHEST, preferred_element_type=F32)
    r_ref[...] = mean
    hi, mid, _ = split3(mean)
    right[...] = jnp.concatenate([hi, mid, hi], axis=0)
    serve(len(steps))
    side_wait(len(steps))
    drain(True)


PLAN = (1, 1, 2, 4, 5, 6, 8, 8, 10, 12)


def low_rank(groups, chips, rows, grads, prev):
    width, local = rows.shape[1], grads.shape[1]
    wide = width // groups
    counts = dict(
        proj=1, zproj=chips - 1, xysum=groups - 1, zsum=chips - 1, zgat=chips - 1, xygat=groups - 1,
        half=groups, zq=chips - 1, qhalf=chips, xyfac=groups - 1, xyfacg=groups - 1,
    )
    dma = [pltpu.SemaphoreType.DMA((counts[s],)) for s in STAGES]
    chunks = 64 // CHUNK
    ring = pltpu.SemaphoreType.DMA((2, chips // 2, chunks))
    side = pltpu.SemaphoreType.DMA((1 + (chips - 1) * chunks,))
    hbm = pl.BlockSpec(memory_space=pl.ANY)
    vmem = pl.BlockSpec(memory_space=pltpu.VMEM)
    return pl.pallas_call(
        functools.partial(main_kernel, groups, chips),
        out_shape=(
            pltpu.VMEM((RANK, width), F32),
            pltpu.VMEM((RANK, local), F32),
            pltpu.VMEM((3 * RANK, width), BF16),
            pltpu.VMEM((3 * RANK, local), BF16),
            pltpu.VMEM((width, local), F32),
            pltpu.VMEM((32 * chips, width), BF16),
            pltpu.VMEM((32 * chips, local), BF16),
        ),
        in_specs=[hbm] * 3,
        out_specs=(vmem,) * 7,
        scratch_shapes=[
            pltpu.VMEM((96 * chips, width), BF16),
            pltpu.VMEM((128 * chips, local), BF16),
            pltpu.VMEM((RANK, local), F32),
            pltpu.VMEM((2, chips, HALF, 128), F32),
            pltpu.VMEM((chips, HALF, 128), F32),
            pltpu.VMEM((chips, HALF, 128), F32),
            pltpu.VMEM((chips - 1, HALF, 128), F32),
            pltpu.VMEM((groups, HALF, wide), F32),
            pltpu.VMEM((groups - 1, HALF, wide), F32),
            pltpu.VMEM((chips, 8, 128), F32),
            pltpu.VMEM((chips - 1, 8, 128), F32),
            pltpu.VMEM((chips, 8, 128), F32),
            pltpu.VMEM((2, groups, HALF, wide), F32),
            pltpu.VMEM((2, chips, HALF, 128), F32),
            pltpu.VMEM((groups, HALF, 128), F32),
            pltpu.VMEM((groups - 1, HALF, 128), F32),
            pltpu.VMEM((groups, HALF, 128), F32),
            *dma,
            *dma,
            ring,
            ring,
            side,
            side,
            pltpu.SemaphoreType.DMA((2 + chips,)),
        ],
        compiler_params=pltpu.CompilerParams(collective_id=0, has_side_effects=True, vmem_limit_bytes=37 << 20),
        name="low_rank",
    )(rows, grads, prev)


def residual_kernel(l_ref, r_ref, left, right, grad_ref, late, late_grads, l_out, r_out, out_ref, block, sems):
    out = [
        pltpu.make_async_copy(l_ref, l_out, sems.at[0]),
        pltpu.make_async_copy(r_ref, r_out, sems.at[1]),
    ]
    for item in out:
        item.start()
    slots, size = block.shape[:2]
    for m in range(grad_ref.shape[0] // size):
        at = slice(m * size, (m + 1) * size)
        if m >= slots:
            out[2 + m - slots].wait()
        rest = dot(late[:, at], late_grads[...], TN) - dot(left[:, at], right[...], TN)
        block[m % slots] = (grad_ref[at] + rest).astype(BF16)
        item = pltpu.make_async_copy(block.at[m % slots], out_ref.at[at], sems.at[2 + m % slots])
        item.start()
        out.append(item)
    for item in out[:2] + out[-slots:]:
        item.wait()


def residual(*parts):
    left, right, _, _, grad, _, _ = parts
    width, local = grad.shape
    size, slots = width // 8, 4
    hbm = pl.BlockSpec(memory_space=pl.ANY)
    vmem = pl.BlockSpec(memory_space=pltpu.VMEM)
    return pl.pallas_call(
        residual_kernel,
        out_shape=(
            jax.ShapeDtypeStruct(left.shape, F32),
            jax.ShapeDtypeStruct(right.shape, F32),
            jax.ShapeDtypeStruct((width, local), BF16),
        ),
        in_specs=[vmem] * 7,
        out_specs=(hbm, hbm, hbm),
        scratch_shapes=[
            pltpu.VMEM((slots, size, local), BF16),
            pltpu.SemaphoreType.DMA((2 + slots,)),
        ],
        compiler_params=pltpu.CompilerParams(vmem_limit_bytes=16 << 20),
        name="residual",
    )(*parts)


def body(groups, chips, activations, out_grads, prev_factor):
    parts = low_rank(groups, chips, activations[0], out_grads[0], prev_factor)
    left, right, rest = residual(*parts)
    return left, right, rest[None]


def solution(mesh):
    placed = (P("dp", "col", None), P("dp", None, "col"), P(None, "col"))
    return jax.shard_map(
        functools.partial(body, mesh.shape["dp"], mesh.shape["col"] // 2),
        mesh=mesh,
        in_specs=placed,
        out_specs=(P(), P(None, "col"), P("dp", None, "col")),
        check_vma=False,
    )
```

```python
import functools
import math

import jax
import jax.numpy as jnp
from jax import lax
from jax.experimental import pallas as pl
from jax.experimental.pallas import tpu as pltpu
from jax.sharding import PartitionSpec as P

MESH = pl.DeviceIdType.MESH
F32 = jnp.float32
BF16 = jnp.bfloat16
RANK = 64
HALF = 32
STAGES = ("proj", "zproj", "xysum", "zsum", "zgat", "xygat", "half", "zq", "qhalf", "xyfac", "xyfacg")
CHUNK = 16


def split3(x):
    hi = x.astype(BF16)
    rest = x - hi.astype(F32)
    mid = rest.astype(BF16)
    lo = (rest - mid.astype(F32)).astype(BF16)
    return hi, mid, lo


def stack3(x):
    return jnp.concatenate(split3(x), axis=0)


def fold3(y, rows):
    return y[:rows] + (y[rows : 2 * rows] + y[2 * rows :])


NN = (((1,), (0,)), ((), ()))
NT = (((1,), (1,)), ((), ()))
TN = (((0,), (0,)), ((), ()))


def dot(a, b, dims):
    return lax.dot_general(a, b, dims, preferred_element_type=F32)


def inverse_factor(gram):
    n = gram.shape[0]
    row = lax.broadcasted_iota(jnp.int32, (n, n), 0)
    column = lax.broadcasted_iota(jnp.int32, (n, n), 1)
    work = jnp.concatenate([jnp.where(row == column, 1.0, 0.0).astype(F32), gram], axis=1)
    out = []
    for top in range(0, n, 8):
        shape = (n - top, 2 * n)
        for p in range(0, 8, 2):
            j = n + top + p
            c0 = jnp.broadcast_to(work[:, j : j + 1], shape)
            c1 = jnp.broadcast_to(work[:, j + 1 : j + 2], shape)
            a, b, d = c0[p : p + 1], c0[p + 1 : p + 2], c1[p + 1 : p + 2]
            over_a = 1.0 / a
            t = b * over_a
            s = d - b * t
            r0 = work[p : p + 1]
            r1 = work[p + 1 : p + 2] - t * r0
            out.append(r0 * lax.rsqrt(a))
            out.append(r1 * lax.rsqrt(s))
            if j + 2 < 2 * n:
                work = work - c0 * (r0 * over_a) - (c1 - c0 * t) * (r1 * (1.0 / s))
        work = work[8:]
    return jnp.concatenate(out, axis=0)[:, :n]


def offsets(chips):
    order = [0]
    for step in range(1, chips // 2):
        order += [chips - step, step]
    return order + [chips // 2]


def main_kernel(
    groups, chips, a_ref, b_ref, p_ref, l_ref, r_ref, left, right, grad_ref, late, late_grads,
    acts, grads, prev, halves, halves_in, psum, psum_in, part, part_in, tile, tile_in, tiles, full, qs, fac, fac_in, facs,
    *sems,
):
    count = len(STAGES)
    send = dict(zip(STAGES, sems[:count]))
    recv = dict(zip(STAGES, sems[count : 2 * count]))
    ring_send, ring_recv, side_send, side_recv, local = sems[2 * count :]
    g = lax.axis_index("dp")
    c = lax.axis_index("col")
    z, k = c // 2, c % 2
    wide = part.shape[2]
    width = acts.shape[1]
    cols = wide // 128
    sibling = (g, 2 * z + (1 - k))
    order = offsets(chips)
    slot_of = {offset: slot for slot, offset in enumerate(order)}

    def chip(offset):
        return lax.rem(z + offset, chips)

    def peer(offset):
        return (g, 2 * chip(offset) + k)

    edge = math.isqrt(groups)
    moves = [(dx, dy) for dx in range(edge) for dy in range(edge)]
    moves.sort(key=lambda move: -sum(min(d, edge - d) for d in move))
    far_first = sorted(range(1, chips), key=lambda i: -min(i, chips - i))

    def group(i, sign=1):
        dx, dy = moves[i - 1]
        x, y = lax.rem(g // edge + sign * dx + edge, edge), lax.rem(lax.rem(g, edge) + sign * dy + edge, edge)
        return x * edge + y

    def copy(stage, slot, src, dst, device):
        return pltpu.make_async_remote_copy(
            src_ref=src, dst_ref=dst, send_sem=send[stage].at[slot], recv_sem=recv[stage].at[slot],
            device_id=device, device_id_type=MESH,
        )

    started = []

    def begin(item):
        item.start()
        started.append(item)
        return item

    def drain(all_of_them=False):
        keep = 0 if all_of_them else 2 * groups
        done = started[: max(0, len(started) - keep)]
        for item in done:
            item.wait_send()
        del started[: len(done)]

    chunks = 64 // CHUNK
    last = chips // 2

    def chunk(slot, core, q, rows=CHUNK):
        early = acts.shape[0] // 128
        ref, slot = (acts, slot) if slot < early else (late, slot - early)
        return ref.at[pl.ds(pl.multiple_of(128 * slot + 64 * core + CHUNK * q, CHUNK), rows)]

    def ring(way, hop, q):
        offset = hop if way else chips - hop
        source = slot_of[(offset - (1 if way else -1)) % chips]
        return pltpu.make_async_remote_copy(
            src_ref=chunk(source, k, q), dst_ref=chunk(slot_of[offset % chips], k, q),
            send_sem=ring_send.at[way, hop - 1, q], recv_sem=ring_recv.at[way, hop - 1, q],
            device_id=peer(chips - 1 if way else 1), device_id_type=MESH,
        )

    steps = []
    for hop in range(1, last):
        steps += [[(0, hop, q), (1, hop, chunks - 1 - q)] for q in range(chunks)]
    steps += [[(0, last, q), (1, last, chunks - 1 - q)] for q in range(chunks // 2)]
    final = {item for step in steps for item in step if item[1] == last}
    served = [0]
    side = []

    def pass_on(slot, q, rows=CHUNK):
        ref = chunk(slot, k, q, rows)
        n = len(side)
        side.append(begin(pltpu.make_async_remote_copy(
            src_ref=ref, dst_ref=ref, send_sem=side_send.at[n], recv_sem=side_recv.at[n],
            device_id=sibling, device_id_type=MESH,
        )))

    ringing = {}

    def serve(upto):
        for step in steps[served[0] : upto]:
            for way, hop, q in step:
                ringing[way, hop, q].wait_recv()
                after = (way, hop + 1, q)
                if hop + 1 < last or after in final:
                    ringing[after] = begin(ring(*after))
            for way, hop, q in step:
                pass_on(slot_of[(hop if way else chips - hop) % chips], q)
        served[0] = max(served[0], upto)

    side_done = [0]

    def side_wait(upto):
        for item in side[side_done[0] : 1 + 2 * upto]:
            item.wait_recv()
        side_done[0] = max(side_done[0], 1 + 2 * upto)

    def multiply(low, high):
        rows = slice(128 * low, 128 * high)
        block = min(1024, width)

        @pl.loop(0, width // block)
        def _(m):
            at = pl.ds(pl.multiple_of(m * block, block), block)
            value = dot(acts[rows, at], grads[rows, :], TN)
            grad_ref[at, :] = value if low == 0 else grad_ref[at, :] + value

    barrier = pltpu.get_barrier_semaphore()
    pl.semaphore_signal(barrier, inc=1, device_id=sibling, device_id_type=MESH)
    for i in range(1, chips):
        pl.semaphore_signal(barrier, inc=1, device_id=peer(i), device_id_type=MESH)
    for i in range(1, groups):
        pl.semaphore_signal(barrier, inc=1, device_id=(group(i), c), device_id_type=MESH)

    loads = [pltpu.make_async_copy(p_ref, prev, local.at[0])]
    for s in range(chips):
        at = pl.ds(pl.multiple_of(128 * chip(order[s]), 128), 128)
        loads.append(pltpu.make_async_copy(b_ref.at[at], grads.at[pl.ds(128 * s, 128)], local.at[1 + s]))
    own = pltpu.make_async_copy(a_ref, acts.at[pl.ds(pl.multiple_of(64 * k, 64), 64)], local.at[1 + chips])
    for item in loads:
        item.start()
    own.start()
    for item in loads:
        item.wait()
    late_grads[...] = grads[96 * chips :]
    proj = fold3(dot(stack3(prev[...]), grads[...], NT), RANK)
    for kk in range(2):
        for s in range(chips):
            halves[kk, s] = proj[HALF * kk : HALF * (kk + 1), 128 * s : 128 * (s + 1)]
    own.wait()
    pl.semaphore_wait(barrier, 1 + (chips - 1) + (groups - 1))

    send_half = begin(copy("proj", 0, halves.at[1 - k], halves_in, sibling))
    pass_on(0, 0, 64)
    for item in steps[0]:
        ringing[item] = begin(ring(*item))
    send_half.wait_recv()

    psum[...] = halves[k] + halves_in[...]
    arriving = [
        begin(copy("zproj", i - 1, psum.at[slot_of[i]], psum_in.at[i - 1], peer(i))) for i in far_first
    ]
    for item in sum(steps[1:chunks], []):
        ringing[item] = begin(ring(*item))
    mine = psum[0]
    for i, item in zip(far_first[::-1], arriving[::-1]):
        item.wait_recv()
        mine = mine + psum_in[i - 1]
    side_wait(0)

    pieces = stack3(mine)
    arriving = []
    for first in range(1, groups + 1, 4):
        batch = range(first, first + 4)
        blocks = [
            fold3(dot(pieces, acts[:128, pl.ds(pl.multiple_of(wide * group(i), wide), wide)], NN), HALF) for i in batch
        ]
        for i, block in zip(batch, blocks):
            part[group(i)] = block
        for i in batch:
            if i < groups:
                arriving.append(
                    begin(copy("xysum", i - 1, part.at[group(i)], part_in.at[i - 1], (group(i), c)))
                )
    serve(PLAN[0])
    mine = part[g]
    for i, item in enumerate(arriving):
        item.wait_recv()
        mine = mine + part_in[i]

    for j in range(chips):
        tile[j] = mine[8 * (j // cols) : 8 * (j // cols + 1), 128 * (j % cols) : 128 * (j % cols + 1)]
    arriving = [begin(copy("zsum", i - 1, tile.at[chip(i)], tile_in.at[i - 1], peer(i))) for i in far_first]
    serve(PLAN[1])
    mine = tile[z]
    for i, item in zip(far_first[::-1], arriving[::-1]):
        item.wait_recv()
        mine = mine + tile_in[i - 1]
    tiles[z] = mine * (1.0 / groups)
    arriving = [begin(copy("zgat", i - 1, tiles.at[z], tiles.at[z], peer(i))) for i in far_first]
    serve(PLAN[2])
    for item in arriving:
        item.wait_recv()
    for j in range(chips):
        full[k, g, 8 * (j // cols) : 8 * (j // cols + 1), 128 * (j % cols) : 128 * (j % cols + 1)] = tiles[j]

    arriving = [begin(copy("xygat", i - 1, full.at[k, g], full.at[k, g], (group(i), c))) for i in range(1, groups)]
    passed = []

    def meet(source):
        at = pl.ds(pl.multiple_of(wide * source, wide), wide)
        return dot(stack3(full[k, source]), acts[:128, at], NT)

    passed.append(begin(copy("half", 0, full.at[k, g], full.at[k, g], sibling)))
    q = meet(g)
    serve(PLAN[3])
    near_first = list(range(groups - 1))[::-1]
    for first in range(0, groups - 1, 4):
        batch = near_first[first : first + 4]
        if first == groups // 2:
            serve(PLAN[4])
        sources = [group(i + 1, -1) for i in batch]
        for i, source in zip(batch, sources):
            arriving[i].wait_recv()
            passed.append(begin(copy("half", i + 1, full.at[k, source], full.at[k, source], sibling)))
        for source in sources:
            q = q + meet(source)
    qs[k, 0] = fold3(q, HALF)

    arriving = [
        begin(copy("zq", i - 1, qs.at[k, 0], qs.at[k, slot_of[chips - i]], peer(i))) for i in far_first
    ]
    crossing = [begin(copy("qhalf", 0, qs.at[k, 0], qs.at[k, 0], sibling))]
    serve(PLAN[5])
    for item in passed:
        item.wait_recv()
    gram = jnp.zeros((RANK, RANK), F32)
    for j in range(groups):
        block = jnp.concatenate([full[0, j], full[1, j]], axis=0)
        gram = gram + lax.dot_general(block, block, NT, precision=lax.Precision.HIGHEST, preferred_element_type=F32)
    inverse = inverse_factor(gram)
    serve(PLAN[6])
    for i, item in zip(far_first[::-1], arriving[::-1]):
        item.wait_recv()
        here = qs.at[k, slot_of[chips - i]]
        crossing.append(begin(copy("qhalf", i, here, here, sibling)))
    for item in crossing:
        item.wait_recv()
    q = jnp.concatenate([jnp.concatenate([qs[0, s], qs[1, s]], axis=0) for s in range(chips)], axis=1)
    factor = fold3(dot(stack3(q), grads[...], NN), RANK)

    tall = factor.shape[1] // 128
    for j in range(groups):
        if j < 2 * tall:
            fac[j] = factor[HALF * (j // tall) : HALF * (j // tall + 1), 128 * (j % tall) : 128 * (j % tall + 1)]
        else:
            fac[j] = jnp.zeros((HALF, 128), F32)
    arriving = [
        begin(copy("xyfac", i - 1, fac.at[group(i)], fac_in.at[i - 1], (group(i), c))) for i in range(1, groups)
    ]
    serve(PLAN[7])
    side_wait(served[0])
    multiply(0, chips // 4)
    serve(9)
    multiply(chips // 4, chips // 2)
    drain()
    serve(PLAN[8])
    mine = fac[g]
    for i, item in enumerate(arriving):
        item.wait_recv()
        mine = mine + fac_in[i]
    facs[g] = mine * (1.0 / groups)
    arriving = [begin(copy("xyfacg", i - 1, facs.at[g], facs.at[g], (group(i), c))) for i in range(1, groups)]
    serve(PLAN[9])
    for j in range(groups):
        block = jnp.concatenate([full[0, j], full[1, j]], axis=0)
        at = slice(wide * j, wide * (j + 1))
        block = lax.dot_general(inverse, block, NN, precision=lax.Precision.HIGHEST, preferred_element_type=F32)
        l_ref[:, at] = block
        hi, mid, _ = split3(block)
        left[:, at] = jnp.concatenate([hi, hi, mid], axis=0)
    side_wait(served[0])
    multiply(chips // 2, 3 * chips // 4)
    drain()
    for item in arriving:
        item.wait_recv()
    mean = jnp.concatenate(
        [jnp.concatenate([facs[tall * h + j] for j in range(tall)], axis=1) for h in range(2)], axis=0
    )
    mean = lax.dot_general(inverse, mean, NN, precision=lax.Precision.HIGHEST, preferred_element_type=F32)
    r_ref[...] = mean
    hi, mid, _ = split3(mean)
    right[...] = jnp.concatenate([hi, mid, hi], axis=0)
    serve(len(steps))
    side_wait(len(steps))
    drain(True)


PLAN = (1, 1, 3, 4, 5, 6, 8, 8, 10, 12)


def low_rank(groups, chips, rows, grads, prev):
    width, local = rows.shape[1], grads.shape[1]
    wide = width // groups
    counts = dict(
        proj=1, zproj=chips - 1, xysum=groups - 1, zsum=chips - 1, zgat=chips - 1, xygat=groups - 1,
        half=groups, zq=chips - 1, qhalf=chips, xyfac=groups - 1, xyfacg=groups - 1,
    )
    dma = [pltpu.SemaphoreType.DMA((counts[s],)) for s in STAGES]
    chunks = 64 // CHUNK
    ring = pltpu.SemaphoreType.DMA((2, chips // 2, chunks))
    side = pltpu.SemaphoreType.DMA((1 + (chips - 1) * chunks,))
    hbm = pl.BlockSpec(memory_space=pl.ANY)
    vmem = pl.BlockSpec(memory_space=pltpu.VMEM)
    return pl.pallas_call(
        functools.partial(main_kernel, groups, chips),
        out_shape=(
            pltpu.VMEM((RANK, width), F32),
            pltpu.VMEM((RANK, local), F32),
            pltpu.VMEM((3 * RANK, width), BF16),
            pltpu.VMEM((3 * RANK, local), BF16),
            pltpu.VMEM((width, local), F32),
            pltpu.VMEM((32 * chips, width), BF16),
            pltpu.VMEM((32 * chips, local), BF16),
        ),
        in_specs=[hbm] * 3,
        out_specs=(vmem,) * 7,
        scratch_shapes=[
            pltpu.VMEM((96 * chips, width), BF16),
            pltpu.VMEM((128 * chips, local), BF16),
            pltpu.VMEM((RANK, local), F32),
            pltpu.VMEM((2, chips, HALF, 128), F32),
            pltpu.VMEM((chips, HALF, 128), F32),
            pltpu.VMEM((chips, HALF, 128), F32),
            pltpu.VMEM((chips - 1, HALF, 128), F32),
            pltpu.VMEM((groups, HALF, wide), F32),
            pltpu.VMEM((groups - 1, HALF, wide), F32),
            pltpu.VMEM((chips, 8, 128), F32),
            pltpu.VMEM((chips - 1, 8, 128), F32),
            pltpu.VMEM((chips, 8, 128), F32),
            pltpu.VMEM((2, groups, HALF, wide), F32),
            pltpu.VMEM((2, chips, HALF, 128), F32),
            pltpu.VMEM((groups, HALF, 128), F32),
            pltpu.VMEM((groups - 1, HALF, 128), F32),
            pltpu.VMEM((groups, HALF, 128), F32),
            *dma,
            *dma,
            ring,
            ring,
            side,
            side,
            pltpu.SemaphoreType.DMA((2 + chips,)),
        ],
        compiler_params=pltpu.CompilerParams(collective_id=0, has_side_effects=True, vmem_limit_bytes=37 << 20),
        name="low_rank",
    )(rows, grads, prev)


def residual_kernel(l_ref, r_ref, left, right, grad_ref, late, late_grads, l_out, r_out, out_ref, block, sems):
    out = [
        pltpu.make_async_copy(l_ref, l_out, sems.at[0]),
        pltpu.make_async_copy(r_ref, r_out, sems.at[1]),
    ]
    for item in out:
        item.start()
    slots, size = block.shape[:2]
    for m in range(grad_ref.shape[0] // size):
        at = slice(m * size, (m + 1) * size)
        if m >= slots:
            out[2 + m - slots].wait()
        rest = dot(late[:, at], late_grads[...], TN) - dot(left[:, at], right[...], TN)
        block[m % slots] = (grad_ref[at] + rest).astype(BF16)
        item = pltpu.make_async_copy(block.at[m % slots], out_ref.at[at], sems.at[2 + m % slots])
        item.start()
        out.append(item)
    for item in out[:2] + out[-slots:]:
        item.wait()


def residual(*parts):
    left, right, _, _, grad, _, _ = parts
    width, local = grad.shape
    size, slots = width // 8, 4
    hbm = pl.BlockSpec(memory_space=pl.ANY)
    vmem = pl.BlockSpec(memory_space=pltpu.VMEM)
    return pl.pallas_call(
        residual_kernel,
        out_shape=(
            jax.ShapeDtypeStruct(left.shape, F32),
            jax.ShapeDtypeStruct(right.shape, F32),
            jax.ShapeDtypeStruct((width, local), BF16),
        ),
        in_specs=[vmem] * 7,
        out_specs=(hbm, hbm, hbm),
        scratch_shapes=[
            pltpu.VMEM((slots, size, local), BF16),
            pltpu.SemaphoreType.DMA((2 + slots,)),
        ],
        compiler_params=pltpu.CompilerParams(vmem_limit_bytes=16 << 20),
        name="residual",
    )(*parts)


def body(groups, chips, activations, out_grads, prev_factor):
    parts = low_rank(groups, chips, activations[0], out_grads[0], prev_factor)
    left, right, rest = residual(*parts)
    return left, right, rest[None]


def solution(mesh):
    placed = (P("dp", "col", None), P("dp", None, "col"), P(None, "col"))
    return jax.shard_map(
        functools.partial(body, mesh.shape["dp"], mesh.shape["col"] // 2),
        mesh=mesh,
        in_specs=placed,
        out_specs=(P(), P(None, "col"), P("dp", None, "col")),
        check_vma=False,
    )
```
